32 devices in a mesh: blk: 16 (over z, x, core), group: 2 (over y).
Axes of the slice: x: 2, y: 2, z: 4, core: 2. Of those that a mesh axis runs over, the one named last changes fastest.
Arguments:
- user_factors: float32 [2, 16384, 256], P('group', 'blk'), may hold values from -1.5 to 1.5
- item_factors: float32 [2, 4096, 256], P('group', 'blk'), may hold values from -1.5 to 1.5
- ratings: bfloat16 [2, 16, 2, 2, 256, 256], P('group', 'blk'), may hold values from -6 to 6
- tile_rows: int32 [2, 16, 2, 2], P('group', 'blk'), may hold values from 0 to 3, as said below
- counts: int32 [2, 16, 2], P('group', 'blk'), may hold values from 0 to 2
- plan: int32 [2, 16], replicated, may hold values from 0 to 15, as said below
Outputs:
- user_out: float32 [2, 16384, 256], P('group', 'blk')
- received: bfloat16 [2, 16, 4, 256, 256], P('group', 'blk')
The draws below stay inside these ranges and needn't reach their ends.
Inputs may be any that keep to these rules, and one draw needn't show every extreme that they name: `tile_rows`: within one stop of one device the 2 entries differ. `plan`: in every group no device receives more than 4 blocks, and some device receives exactly 4.
All inputs are finite; a program needn't handle non-finite values.
Results may differ from the reference program's by a relative error of at most 0.006.
Values may be sent and summed in bfloat16 or wider, within the bound.
A program may use at most 64 MiB of HBM per device.

```python
import jax
import jax.numpy as jnp
from jax import lax

R = 256
TILE = 256
UB = 1024
CAPT = 2
CAP = 4
IB = 256
BLOCKS = 16
GROUPS = 2
STOPS = 2
USERS = 16384
ITEMS = 4096


def factor_draw(key, rows):
    return 0.25 * jax.random.truncated_normal(key, -6.0, 6.0, (GROUPS, rows, R), jnp.float32)


def draw_user_factors(key, part):
    return factor_draw(jax.random.fold_in(key, 11), USERS)


def draw_item_factors(key, part):
    return factor_draw(jax.random.fold_in(key, 23), ITEMS)


def draw_tile_rows(key, part):
    rows_per = UB // TILE
    scores = jax.random.randint(key, (GROUPS, BLOCKS, STOPS, rows_per), 0, 1 << 20) * rows_per + jnp.arange(rows_per)
    ranked = jnp.argsort(scores, axis=-1, stable=True).astype(jnp.int32)
    return ranked[..., :CAPT]


def draw_plan(key, part):

    def one_group(group_id):
        group_key = jax.random.fold_in(key, group_id)
        first_key, second_key = jax.random.split(group_key)
        block_order = jax.random.permutation(first_key, BLOCKS)
        devices = jax.random.permutation(second_key, BLOCKS)
        positions = jnp.arange(BLOCKS)
        device_slot = jnp.where(positions < CAP, 0, 1 + (positions - CAP) // 2)
        targets = devices[device_slot]
        return jnp.zeros((BLOCKS,), jnp.int32).at[block_order].set(targets.astype(jnp.int32))
    return jax.vmap(one_group)(jnp.arange(GROUPS)).astype(jnp.int32)


def place_ends(values, stream_key, least, high):
    place = [jax.random.randint(jax.random.fold_in(stream_key, axis), (), 0, length) for axis, length in enumerate(values.shape)]
    main_axis = values.shape.index(max(values.shape))
    neighbour = place[:main_axis] + [(place[main_axis] + 1) % values.shape[main_axis]] + place[main_axis + 1:]
    return values.at[tuple(place)].set(least).at[tuple(neighbour)].set(high)


def block_levels(stream_key, extent, pieces, smallest, largest):
    def one(dim, parts):
        draws = jax.random.uniform(jax.random.fold_in(jax.random.fold_in(stream_key, 6), dim), (parts,), jnp.float32, smallest / len(pieces), largest / len(pieces))
        return jnp.repeat(jnp.exp(draws), extent[dim] // parts).reshape((-1,) + (1,) * (len(extent) - dim - 1))

    loudness = one(*pieces[0])
    for cut in pieces[1:]:
        loudness = loudness * one(*cut)
    return loudness


def scatter_about(key, shape, width, most, pieces=(), dtype=jnp.bfloat16):
    values = jax.random.normal(key, shape, jnp.float32) * width
    if len(pieces) > 0:
        values = block_levels(key, shape, pieces, -0.22, 0.18) * values
    return jnp.clip(values, min=-most, max=most).astype(dtype)


def setup_inputs(seed: int = 0) -> dict:
    seeds = jax.random.split(jax.random.key(seed), 7)
    user_factors = draw_user_factors(jax.random.fold_in(seeds[6], 71), 0)
    item_factors = draw_item_factors(jax.random.fold_in(seeds[6], 71), 0)
    ratings = scatter_about(seeds[2], (GROUPS, BLOCKS, STOPS, CAPT, TILE, TILE), 1.0, 6.0, ((0, 2), (1, 16)))
    tile_rows = draw_tile_rows(jax.random.fold_in(seeds[6], 71), 0)
    counts = place_ends(jax.random.randint(seeds[4], (GROUPS, BLOCKS, STOPS), 0, CAPT + 1), jax.random.fold_in(seeds[4], 1), 0, CAPT).astype(jnp.int32)
    plan = draw_plan(jax.random.fold_in(seeds[6], 71), 0)
    return {"user_factors": user_factors, "item_factors": item_factors, "ratings": ratings, "tile_rows": tile_rows, "counts": counts, "plan": plan}


learn_rate = 0.01
shrinkage = 0.05


def round_trip(values):
    return lax.optimization_barrier(values.astype(jnp.bfloat16)).astype(jnp.float32)


def reference(user_factors, item_factors, ratings, tile_rows, counts, plan):
    rows_per = UB // TILE
    user_rows = user_factors.reshape(GROUPS, BLOCKS, rows_per, TILE, R)
    item_block = item_factors.reshape(GROUPS, BLOCKS, IB, R)
    slot_ids = jnp.arange(CAPT)
    for stop_index in range(STOPS):
        if stop_index > 0:
            item_block = jnp.roll(item_block, 1, axis=1)
        selector = (tile_rows[:, :, stop_index, :, None] == jnp.arange(rows_per)[None, None, None, :]).astype(jnp.float32)
        before = jnp.einsum("gbcr,gbrtk->gbctk", selector, user_rows, precision=lax.Precision.HIGHEST)
        active = (slot_ids[None, None, :] < counts[:, :, stop_index, None]).astype(jnp.float32)
        user_low = round_trip(before)
        item_low = round_trip(item_block)
        predicted = jnp.einsum("gbctk,gbik->gbcti", user_low, item_low)
        residual = round_trip(active[..., None, None] * (ratings[:, :, stop_index].astype(jnp.float32) - predicted))
        change = learn_rate * active[..., None, None] * (jnp.einsum("gbcti,gbik->gbctk", residual, item_low) - shrinkage * before)
        user_rows = user_rows + jnp.einsum("gbcr,gbctk->gbrtk", selector, change, precision=lax.Precision.HIGHEST)
        grad_items = jnp.einsum("gbcti,gbctk->gbik", residual, user_low)
        tile_count = counts[:, :, stop_index, None, None].astype(jnp.float32)
        item_block = item_block + learn_rate * (grad_items - shrinkage * tile_count * item_block)
    at_home = jnp.roll(item_block, -(STOPS - 1), axis=1)
    handed = round_trip(at_home)
    positions = jnp.arange(BLOCKS)
    same_dest = plan[:, :, None] == plan[:, None, :]
    earlier = positions[None, None, :] < positions[None, :, None]
    slot_of = jnp.sum((same_dest & earlier).astype(jnp.int32), axis=2)
    selector = ((plan[:, None, None, :] == positions[None, :, None, None]) & (slot_of[:, None, None, :] == jnp.arange(CAP)[None, None, :, None])).astype(jnp.float32)
    shifted = jnp.einsum("gdck,gkir->gdcir", selector, handed, precision=lax.Precision.HIGHEST).astype(jnp.bfloat16)
    received = jnp.roll(shifted, 1, axis=0)
    return user_rows.reshape(GROUPS, USERS, R), received
```

```python
import functools

import jax
import jax.numpy as jnp
from jax import lax
from jax.experimental import pallas as pl
from jax.experimental.pallas import tpu as pltpu
from jax.sharding import PartitionSpec as P

CAP = 4
PARTS = 2

learn_rate = 0.01
shrinkage = 0.05

MESH = pl.DeviceIdType.MESH
F32 = jnp.float32
LOW = jnp.bfloat16


def kernel(
    blocks, groups, parts,
    users, items, ratings, row_table, count_table, plan,
    users_out, received,
    ring_out, ring_in, handed, gathered, staged, change, picks,
    ring_send, ring_recv, part_send, part_recv, slot_send, slot_recv, own_sem,
):
    stops, capt = ratings.shape[0], ratings.shape[1]
    tiles = users.shape[0]
    lanes = blocks // parts
    depth = gathered.shape[1]
    me = lax.axis_index("blk")
    group = lax.axis_index("group")
    ahead, behind = lax.rem(group + 1, groups), lax.rem(group + groups - 1, groups)
    right, left = lax.rem(me + 1, blocks), lax.rem(me + blocks - 1, blocks)
    part_first = (me // lanes) * lanes
    lane = me - part_first

    barrier = pltpu.get_barrier_semaphore()
    pl.semaphore_signal(barrier, inc=1, device_id=(left, group), device_id_type=MESH)
    for step in range(blocks):
        pl.semaphore_signal(
            barrier, inc=1, device_id=(lax.rem(me + step, blocks), behind), device_id_type=MESH
        )
    for step in range(1, lanes):
        other = part_first + lax.rem(lane + step, lanes)
        pl.semaphore_signal(barrier, inc=1, device_id=(other, group), device_id_type=MESH)

    change[capt] = jnp.zeros(change.shape[1:], F32)
    gathered[blocks] = jnp.zeros(gathered.shape[1:], LOW)

    def ring_copy(stop, half):
        return pltpu.make_async_remote_copy(
            src_ref=ring_out.at[stop, half],
            dst_ref=ring_in.at[stop, half],
            send_sem=ring_send.at[stop, half],
            recv_sem=ring_recv.at[stop, half],
            device_id=(right, group),
            device_id_type=MESH,
        )

    def part_copy(step):
        target = lax.rem(me + step, blocks)
        first = pl.multiple_of(lax.rem(target, lanes) * depth, depth)
        return pltpu.make_async_remote_copy(
            src_ref=handed.at[pl.ds(first, depth)],
            dst_ref=gathered.at[me],
            send_sem=part_send.at[step],
            recv_sem=part_recv.at[me],
            device_id=(target, ahead),
            device_id_type=MESH,
        )

    rows_here = pl.ds(pl.multiple_of(lane * depth, depth), depth)

    def slot_copy(step):
        return pltpu.make_async_remote_copy(
            src_ref=staged.at[step],
            dst_ref=received.at[:, rows_here],
            send_sem=slot_send.at[step],
            recv_sem=slot_recv.at[lane],
            device_id=(part_first + lax.rem(lane + step, lanes), group),
            device_id_type=MESH,
        )

    for stop in range(stops):
        source = users if stop == 0 else users_out
        count = count_table[stop]
        if stop == 0:
            item_low = items[...].astype(LOW)
        else:
            ring_copy(stop - 1, 0).wait_recv()
            item_low = ring_in[stop - 1, 0]
        grad = jnp.zeros(items.shape, F32)
        kept = []
        for c in range(capt):
            active = (c < count).astype(F32)
            before = source[row_table[stop, c]]
            user_low = before.astype(LOW)
            predicted = lax.dot_general(
                user_low, item_low, (((1,), (1,)), ((), ())), preferred_element_type=F32
            )
            residual = (active * (ratings[stop, c].astype(F32) - predicted)).astype(LOW)
            grad = grad + lax.dot_general(
                residual, user_low, (((0,), (0,)), ((), ())), preferred_element_type=F32
            )
            kept.append((active, residual))
        if stop == 0:
            block = items[...]
        else:
            ring_copy(stop - 1, 1).wait_recv()
            block = ring_in[stop - 1, 0].astype(F32) + ring_in[stop - 1, 1].astype(F32)
        block = block + learn_rate * (grad - shrinkage * count.astype(F32) * block)
        if stop == 0:
            pl.semaphore_wait(barrier, blocks + lanes)
        if stop < stops - 1:
            high = block.astype(LOW)
            ring_out[stop, 0] = high
            ring_copy(stop, 0).start()
            ring_out[stop, 1] = (block - high.astype(F32)).astype(LOW)
            ring_copy(stop, 1).start()
        else:
            handed[...] = block.astype(LOW)
            for step in range(blocks):
                part_copy(step).start()
        for c in range(capt):
            active, residual = kept[c]
            before = source[row_table[stop, c]]
            user_step = jnp.dot(residual, item_low, preferred_element_type=F32)
            change[c] = learn_rate * active * (user_step - shrinkage * before)
        for tile in range(tiles):
            which = jnp.int32(capt)
            for c in range(capt):
                which = jnp.where(row_table[stop, c] == tile, c, which)
            users_out[tile] = source[tile] + change[which]

    def find(step, carry):
        target = part_first + lax.rem(lane + step, lanes)
        seen = jnp.int32(0)
        found = [jnp.int32(blocks)] * CAP
        for k in range(blocks):
            match = plan[behind, k] == target
            for c in range(CAP):
                found[c] = jnp.where(match & (seen == c), k, found[c])
            seen = seen + match.astype(jnp.int32)
        for c in range(CAP):
            picks[step, c] = found[c]
        return carry

    lax.fori_loop(0, lanes, find, 0)

    for k in range(blocks):
        pltpu.make_async_remote_copy(
            src_ref=gathered.at[k],
            dst_ref=gathered.at[k],
            send_sem=part_send.at[k],
            recv_sem=part_recv.at[k],
            device_id=(k, behind),
            device_id_type=MESH,
        ).wait_recv()

    def held_by(k):
        place = lax.rem(k + (stops - 1), blocks)
        return jnp.where(k == blocks, blocks, place)

    for step in list(range(1, lanes)) + [0]:
        for c in range(CAP):
            staged[step, c] = gathered[held_by(picks[step, c])]
        if step > 0:
            slot_copy(step).start()
    own = pltpu.make_async_copy(staged.at[0], received.at[:, rows_here], own_sem)
    own.start()
    own.wait()
    for step in range(1, lanes):
        sender = lax.rem(lane + step, lanes)
        rows = pl.ds(pl.multiple_of(sender * depth, depth), depth)
        pltpu.make_async_remote_copy(
            src_ref=staged.at[step],
            dst_ref=received.at[:, rows],
            send_sem=slot_send.at[step],
            recv_sem=slot_recv.at[sender],
            device_id=(part_first + sender, group),
            device_id_type=MESH,
        ).wait_recv()
    for step in range(1, lanes):
        slot_copy(step).wait_send()
    for step in range(blocks):
        part_copy(step).wait_send()
    for stop in range(stops - 1):
        for half in range(2):
            ring_copy(stop, half).wait_send()


def shards(user_factors, item_factors, ratings, tile_rows, counts, plan):
    blocks, groups = lax.axis_size("blk"), lax.axis_size("group")
    _, _, stops, capt, tile, _ = ratings.shape
    _, rows, rank = user_factors.shape
    depth_all = item_factors.shape[1]
    parts = max(PARTS, blocks * 16 // depth_all)
    lanes = blocks // parts
    depth = depth_all // lanes
    vmem = pl.BlockSpec(memory_space=pltpu.VMEM)
    smem = pl.BlockSpec(memory_space=pltpu.SMEM)
    hops = max(stops - 1, 1)
    users, received = pl.pallas_call(
        functools.partial(kernel, blocks, groups, parts),
        out_shape=(
            jax.ShapeDtypeStruct((rows // tile, tile, rank), F32),
            jax.ShapeDtypeStruct((CAP, depth_all, rank), LOW),
        ),
        in_specs=[vmem, vmem, vmem, smem, smem, smem],
        out_specs=(vmem, vmem),
        scratch_shapes=[
            pltpu.VMEM((hops, 2, depth_all, rank), LOW),
            pltpu.VMEM((hops, 2, depth_all, rank), LOW),
            pltpu.VMEM((depth_all, rank), LOW),
            pltpu.VMEM((blocks + 1, depth, rank), LOW),
            pltpu.VMEM((lanes, CAP, depth, rank), LOW),
            pltpu.VMEM((capt + 1, tile, rank), F32),
            pltpu.SMEM((lanes, CAP), jnp.int32),
            pltpu.SemaphoreType.DMA((hops, 2)),
            pltpu.SemaphoreType.DMA((hops, 2)),
            pltpu.SemaphoreType.DMA((blocks,)),
            pltpu.SemaphoreType.DMA((blocks,)),
            pltpu.SemaphoreType.DMA((lanes,)),
            pltpu.SemaphoreType.DMA((lanes,)),
            pltpu.SemaphoreType.DMA,
        ],
        compiler_params=pltpu.CompilerParams(
            collective_id=0, has_side_effects=True, vmem_limit_bytes=48 * 1024 * 1024
        ),
        cost_estimate=pl.CostEstimate(
            flops=6 * stops * capt * tile * depth_all * rank,
            bytes_accessed=2 * rows * rank * 4,
            transcendentals=0,
        ),
    )(
        user_factors.reshape(rows // tile, tile, rank),
        item_factors[0],
        ratings[0, 0],
        tile_rows[0, 0],
        counts[0, 0],
        plan,
    )
    return users.reshape(1, rows, rank), received[None, None]


def solution(mesh):
    in_specs = (
        P("group", "blk", None),
        P("group", "blk", None),
        P("group", "blk", None, None, None, None),
        P("group", "blk", None, None),
        P("group", "blk", None),
        P(),
    )
    out_specs = (P("group", "blk", None), P("group", "blk", None, None, None))
    return jax.shard_map(shards, mesh=mesh, in_specs=in_specs, out_specs=out_specs, check_vma=False)
```

```python
import functools

import jax
import jax.numpy as jnp
from jax import lax
from jax.experimental import pallas as pl
from jax.experimental.pallas import tpu as pltpu
from jax.sharding import PartitionSpec as P

CAP = 4
PARTS = 2
CHUNKS = 2
VMEM_GRANT = 63 * 1024 * 1024

learn_rate = 0.01
shrinkage = 0.05

MESH = pl.DeviceIdType.MESH
F32 = jnp.float32
LOW = jnp.bfloat16


def kernel(
    blocks, groups, parts, chunks,
    users_hbm, items_hbm, ratings_hbm, row_table, count_table, plan,
    users_out, received,
    users, items, ratings, ring_out, ring_in, handed, staged, change, picks,
    load_sem, ring_send, ring_recv, part_send, part_recv, slot_send, slot_recv, own_sem, out_sem,
    *gathered,
):
    stops, capt = ratings.shape[0], ratings.shape[1]
    tiles = users.shape[0]
    lanes = blocks // parts
    depth = gathered[0].shape[1]
    width = depth * lanes
    me = lax.axis_index("blk")
    group = lax.axis_index("group")
    ahead, behind = lax.rem(group + 1, groups), lax.rem(group + groups - 1, groups)
    right, left = lax.rem(me + 1, blocks), lax.rem(me + blocks - 1, blocks)
    part_first = (me // lanes) * lanes
    lane = me - part_first

    loads = [pltpu.make_async_copy(items_hbm, items, load_sem.at[0])]
    loads.append(pltpu.make_async_copy(users_hbm, users, load_sem.at[1]))
    for stop in range(stops):
        loads.append(
            pltpu.make_async_copy(ratings_hbm.at[stop], ratings.at[stop], load_sem.at[2 + stop])
        )
    for load in loads:
        load.start()

    barrier = pltpu.get_barrier_semaphore()
    pl.semaphore_signal(barrier, inc=1, device_id=(left, group), device_id_type=MESH)
    for step in range(blocks):
        pl.semaphore_signal(
            barrier, inc=1, device_id=(lax.rem(me + step, blocks), behind), device_id_type=MESH
        )
    for step in range(1, lanes):
        other = part_first + lax.rem(lane + step, lanes)
        pl.semaphore_signal(barrier, inc=1, device_id=(other, group), device_id_type=MESH)

    change[capt] = jnp.zeros(change.shape[1:], F32)
    for chunk in range(chunks):
        gathered[chunk][blocks] = jnp.zeros(gathered[chunk].shape[1:], LOW)

    def ring_copy(stop, chunk, half):
        return pltpu.make_async_remote_copy(
            src_ref=ring_out.at[stop, chunk, half],
            dst_ref=ring_in.at[stop, chunk, half],
            send_sem=ring_send.at[stop, chunk, half],
            recv_sem=ring_recv.at[stop, chunk, half],
            device_id=(right, group),
            device_id_type=MESH,
        )

    def part_copy(chunk, step):
        target = lax.rem(me + step, blocks)
        first = pl.multiple_of(lax.rem(target, lanes) * depth, depth)
        return pltpu.make_async_remote_copy(
            src_ref=handed.at[chunk, pl.ds(first, depth)],
            dst_ref=gathered[chunk].at[me],
            send_sem=part_send.at[chunk, step],
            recv_sem=part_recv.at[chunk, me],
            device_id=(target, ahead),
            device_id_type=MESH,
        )

    def slot_rows(chunk, holder):
        return pl.ds(pl.multiple_of(chunk * width + holder * depth, depth), depth)

    def slot_copy(chunk, step):
        return pltpu.make_async_remote_copy(
            src_ref=staged.at[chunk, step],
            dst_ref=received.at[:, slot_rows(chunk, lane)],
            send_sem=slot_send.at[chunk, step],
            recv_sem=slot_recv.at[chunk, lane],
            device_id=(part_first + lax.rem(lane + step, lanes), group),
            device_id_type=MESH,
        )

    loads[0].wait()
    loads[1].wait()
    for stop in range(stops):
        loads[2 + stop].wait()
        count = count_table[stop]
        active = [(c < count).astype(F32) for c in range(capt)]
        user_low = [users[row_table[stop, c]].astype(LOW) for c in range(capt)]
        kept = []
        for chunk in range(chunks):
            rows = slice(chunk * width, (chunk + 1) * width)
            if stop == 0:
                item_low = items[rows].astype(LOW)
            else:
                ring_copy(stop - 1, chunk, 0).wait_recv()
                item_low = ring_in[stop - 1, chunk, 0]
            grad = jnp.zeros((width, items.shape[1]), F32)
            residuals = []
            for c in range(capt):
                predicted = lax.dot_general(
                    user_low[c], item_low, (((1,), (1,)), ((), ())), preferred_element_type=F32
                )
                residual = (
                    active[c] * (ratings[stop, c, :, rows].astype(F32) - predicted)
                ).astype(LOW)
                grad = grad + lax.dot_general(
                    residual, user_low[c], (((0,), (0,)), ((), ())), preferred_element_type=F32
                )
                residuals.append(residual)
            kept.append((item_low, residuals))
            if stop == 0:
                block = items[rows]
            else:
                ring_copy(stop - 1, chunk, 1).wait_recv()
                block = item_low.astype(F32) + ring_in[stop - 1, chunk, 1].astype(F32)
            block = block + learn_rate * (grad - shrinkage * count.astype(F32) * block)
            if stop == 0 and chunk == 0:
                pl.semaphore_wait(barrier, blocks + lanes)
            if stop < stops - 1:
                high = block.astype(LOW)
                ring_out[stop, chunk, 0] = high
                ring_copy(stop, chunk, 0).start()
                ring_out[stop, chunk, 1] = (block - high.astype(F32)).astype(LOW)
                ring_copy(stop, chunk, 1).start()
            else:
                handed[chunk] = block.astype(LOW)
                for step in range(blocks):
                    part_copy(chunk, step).start()
        for c in range(capt):
            before = users[row_table[stop, c]]
            user_step = jnp.zeros(before.shape, F32)
            for item_low, residuals in kept:
                user_step = user_step + jnp.dot(
                    residuals[c], item_low, preferred_element_type=F32
                )
            change[c] = learn_rate * active[c] * (user_step - shrinkage * before)
        for tile in range(tiles):
            which = jnp.int32(capt)
            for c in range(capt):
                which = jnp.where(row_table[stop, c] == tile, c, which)
            users[tile] = users[tile] + change[which]
    save = pltpu.make_async_copy(users, users_out, out_sem)
    save.start()

    def find(step, carry):
        target = part_first + lax.rem(lane + step, lanes)
        seen = jnp.int32(0)
        found = [jnp.int32(blocks)] * CAP
        for k in range(blocks):
            match = plan[behind, k] == target
            for c in range(CAP):
                found[c] = jnp.where(match & (seen == c), (k + stops - 1) % blocks, found[c])
            seen = seen + match.astype(jnp.int32)
        for c in range(CAP):
            picks[step, c] = found[c]
        return carry

    lax.fori_loop(0, lanes, find, 0)

    own = []
    for chunk in range(chunks):
        for k in range(blocks):
            pltpu.make_async_remote_copy(
                src_ref=gathered[chunk].at[k],
                dst_ref=gathered[chunk].at[k],
                send_sem=part_send.at[chunk, k],
                recv_sem=part_recv.at[chunk, k],
                device_id=(k, behind),
                device_id_type=MESH,
            ).wait_recv()
        for step in list(range(1, lanes)) + [0]:
            for c in range(CAP):
                staged[chunk, step, c] = gathered[chunk][picks[step, c]]
            if step > 0:
                slot_copy(chunk, step).start()
        own.append(
            pltpu.make_async_copy(
                staged.at[chunk, 0], received.at[:, slot_rows(chunk, lane)], own_sem.at[chunk]
            )
        )
        own[-1].start()
    for chunk in range(chunks):
        for step in range(1, lanes):
            sender = lax.rem(lane + step, lanes)
            pltpu.make_async_remote_copy(
                src_ref=staged.at[chunk, step],
                dst_ref=received.at[:, slot_rows(chunk, sender)],
                send_sem=slot_send.at[chunk, step],
                recv_sem=slot_recv.at[chunk, sender],
                device_id=(part_first + sender, group),
                device_id_type=MESH,
            ).wait_recv()
    for chunk in range(chunks):
        own[chunk].wait()
        for step in range(1, lanes):
            slot_copy(chunk, step).wait_send()
        for step in range(blocks):
            part_copy(chunk, step).wait_send()
        for stop in range(stops - 1):
            for half in range(2):
                ring_copy(stop, chunk, half).wait_send()
    save.wait()


def shards(user_factors, item_factors, ratings, tile_rows, counts, plan):
    blocks, groups = lax.axis_size("blk"), lax.axis_size("group")
    _, _, stops, capt, tile, _ = ratings.shape
    _, rows, rank = user_factors.shape
    item_rows = item_factors.shape[1]
    parts = max(PARTS, blocks * 16 // item_rows)
    lanes = blocks // parts
    chunks = max(1, min(CHUNKS, item_rows // (lanes * 16)))
    width = item_rows // chunks
    depth = width // lanes
    tiled = (rows // tile, tile, rank)
    hbm = pl.BlockSpec(memory_space=pltpu.HBM)
    smem = pl.BlockSpec(memory_space=pltpu.SMEM)
    place = pl.BlockSpec(memory_space=pl.ANY)
    hops = max(stops - 1, 1)
    users, received = pl.pallas_call(
        functools.partial(kernel, blocks, groups, parts, chunks),
        out_shape=(
            jax.ShapeDtypeStruct(tiled, F32),
            jax.ShapeDtypeStruct((CAP, item_rows, rank), LOW),
        ),
        in_specs=[hbm, hbm, hbm, smem, smem, smem],
        out_specs=(place, place),
        scratch_shapes=[
            pltpu.VMEM(tiled, F32),
            pltpu.VMEM((item_rows, rank), F32),
            pltpu.VMEM(ratings.shape[2:], LOW),
            pltpu.VMEM((hops, chunks, 2, width, rank), LOW),
            pltpu.VMEM((hops, chunks, 2, width, rank), LOW),
            pltpu.VMEM((chunks, width, rank), LOW),
            pltpu.VMEM((chunks, lanes, CAP, depth, rank), LOW),
            pltpu.VMEM((capt + 1, tile, rank), F32),
            pltpu.SMEM((lanes, CAP), jnp.int32),
            pltpu.SemaphoreType.DMA((2 + stops,)),
            pltpu.SemaphoreType.DMA((hops, chunks, 2)),
            pltpu.SemaphoreType.DMA((hops, chunks, 2)),
            pltpu.SemaphoreType.DMA((chunks, blocks)),
            pltpu.SemaphoreType.DMA((chunks, blocks)),
            pltpu.SemaphoreType.DMA((chunks, lanes)),
            pltpu.SemaphoreType.DMA((chunks, lanes)),
            pltpu.SemaphoreType.DMA((chunks,)),
            pltpu.SemaphoreType.DMA,
        ]
        + [pltpu.VMEM((blocks + 1, depth, rank), LOW)] * chunks,
        compiler_params=pltpu.CompilerParams(
            collective_id=0, has_side_effects=True, vmem_limit_bytes=VMEM_GRANT
        ),
        cost_estimate=pl.CostEstimate(
            flops=6 * stops * capt * tile * item_rows * rank,
            bytes_accessed=2 * rows * rank * 4,
            transcendentals=0,
        ),
    )(
        user_factors.reshape(tiled),
        item_factors[0],
        ratings[0, 0],
        tile_rows[0, 0],
        counts[0, 0],
        plan,
    )
    return users.reshape(1, rows, rank), received[None, None]


def solution(mesh):
    in_specs = (
        P("group", "blk", None),
        P("group", "blk", None),
        P("group", "blk", None, None, None, None),
        P("group", "blk", None, None),
        P("group", "blk", None),
        P(),
    )
    out_specs = (P("group", "blk", None), P("group", "blk", None, None, None))
    return jax.shard_map(shards, mesh=mesh, in_specs=in_specs, out_specs=out_specs, check_vma=False)
```

```python
import functools

import jax
import jax.numpy as jnp
from jax import lax
from jax.experimental import pallas as pl
from jax.experimental.pallas import tpu as pltpu
from jax.sharding import PartitionSpec as P

CAP = 4
PARTS = 2
CHUNKS = 2
VMEM_GRANT = 63 * 1024 * 1024

learn_rate = 0.01
shrinkage = 0.05

MESH = pl.DeviceIdType.MESH
F32 = jnp.float32
LOW = jnp.bfloat16


def kernel(
    blocks, groups, parts, chunks,
    users_hbm, items_hbm, ratings_hbm, row_table, count_table, plan,
    users_out, received,
    users, items, ratings, ring_out, ring_in, handed, staged, change, picks,
    load_sem, ring_send, ring_recv, part_send, part_recv, slot_send, slot_recv, own_sem, out_sem,
    *gathered,
):
    stops, capt = ratings.shape[0], ratings.shape[1]
    tiles = users.shape[0]
    lanes = blocks // parts
    depth = gathered[0].shape[1]
    width = depth * lanes
    me = lax.axis_index("blk")
    group = lax.axis_index("group")
    ahead, behind = lax.rem(group + 1, groups), lax.rem(group + groups - 1, groups)
    right, left = lax.rem(me + 1, blocks), lax.rem(me + blocks - 1, blocks)
    part_first = (me // lanes) * lanes
    lane = me - part_first

    loads = [pltpu.make_async_copy(items_hbm, items, load_sem.at[0])]
    loads.append(pltpu.make_async_copy(users_hbm, users, load_sem.at[1]))
    for stop in range(stops):
        loads.append(
            pltpu.make_async_copy(ratings_hbm.at[stop], ratings.at[stop], load_sem.at[2 + stop])
        )
    for load in loads:
        load.start()

    barrier = pltpu.get_barrier_semaphore()
    pl.semaphore_signal(barrier, inc=1, device_id=(left, group), device_id_type=MESH)
    for step in range(blocks):
        pl.semaphore_signal(
            barrier, inc=1, device_id=(lax.rem(me + step, blocks), behind), device_id_type=MESH
        )
    for step in range(1, lanes):
        other = part_first + lax.rem(lane + step, lanes)
        pl.semaphore_signal(barrier, inc=1, device_id=(other, group), device_id_type=MESH)

    change[capt] = jnp.zeros(change.shape[1:], F32)
    for chunk in range(chunks):
        gathered[chunk][blocks] = jnp.zeros(gathered[chunk].shape[1:], LOW)

    def ring_copy(stop, chunk, half):
        return pltpu.make_async_remote_copy(
            src_ref=ring_out.at[stop, chunk, half],
            dst_ref=ring_in.at[stop, chunk, half],
            send_sem=ring_send.at[stop, chunk, half],
            recv_sem=ring_recv.at[stop, chunk, half],
            device_id=(right, group),
            device_id_type=MESH,
        )

    def part_copy(chunk, step):
        target = lax.rem(me + step, blocks)
        first = pl.multiple_of(lax.rem(target, lanes) * depth, depth)
        return pltpu.make_async_remote_copy(
            src_ref=handed.at[chunk, pl.ds(first, depth)],
            dst_ref=gathered[chunk].at[me],
            send_sem=part_send.at[chunk, step],
            recv_sem=part_recv.at[chunk, me],
            device_id=(target, ahead),
            device_id_type=MESH,
        )

    def slot_rows(chunk, holder):
        return pl.ds(pl.multiple_of(chunk * width + holder * depth, depth), depth)

    def slot_copy(chunk, step):
        return pltpu.make_async_remote_copy(
            src_ref=staged.at[chunk, step],
            dst_ref=received.at[:, slot_rows(chunk, lane)],
            send_sem=slot_send.at[chunk, step],
            recv_sem=slot_recv.at[chunk, lane],
            device_id=(part_first + lax.rem(lane + step, lanes), group),
            device_id_type=MESH,
        )

    loads[0].wait()
    loads[1].wait()
    for stop in range(stops):
        loads[2 + stop].wait()
        count = count_table[stop]
        active = [(c < count).astype(F32) for c in range(capt)]
        user_low = [users[row_table[stop, c]].astype(LOW) for c in range(capt)]
        kept = []
        for chunk in range(chunks):
            rows = slice(chunk * width, (chunk + 1) * width)
            if stop == 0:
                item_low = items[rows].astype(LOW)
            else:
                ring_copy(stop - 1, chunk, 0).wait_recv()
                item_low = ring_in[stop - 1, chunk, 0]
            grad = jnp.zeros((width, items.shape[1]), F32)
            residuals = []
            for c in range(capt):
                predicted = lax.dot_general(
                    user_low[c], item_low, (((1,), (1,)), ((), ())), preferred_element_type=F32
                )
                residual = (
                    active[c] * (ratings[stop, c, :, rows].astype(F32) - predicted)
                ).astype(LOW)
                grad = grad + lax.dot_general(
                    residual, user_low[c], (((0,), (0,)), ((), ())), preferred_element_type=F32
                )
                residuals.append(residual)
            kept.append((item_low, residuals))
            if stop == 0:
                block = items[rows]
            else:
                ring_copy(stop - 1, chunk, 1).wait_recv()
                block = item_low.astype(F32) + ring_in[stop - 1, chunk, 1].astype(F32)
            block = block + learn_rate * (grad - shrinkage * count.astype(F32) * block)
            if stop == 0 and chunk == 0:
                pl.semaphore_wait(barrier, blocks + lanes)
            if stop < stops - 1:
                high = block.astype(LOW)
                ring_out[stop, chunk, 0] = high
                ring_copy(stop, chunk, 0).start()
                ring_out[stop, chunk, 1] = (block - high.astype(F32)).astype(LOW)
                ring_copy(stop, chunk, 1).start()
            else:
                handed[chunk] = block.astype(LOW)
                for step in range(blocks):
                    part_copy(chunk, step).start()
        for c in range(capt):
            before = users[row_table[stop, c]]
            user_step = jnp.zeros(before.shape, F32)
            for item_low, residuals in kept:
                user_step = user_step + jnp.dot(
                    residuals[c], item_low, preferred_element_type=F32
                )
            change[c] = learn_rate * active[c] * (user_step - shrinkage * before)
        for tile in range(tiles):
            which = jnp.int32(capt)
            for c in range(capt):
                which = jnp.where(row_table[stop, c] == tile, c, which)
            users[tile] = users[tile] + change[which]
    save = pltpu.make_async_copy(users, users_out, out_sem)
    save.start()

    def find(step, carry):
        target = part_first + lax.rem(lane + step, lanes)
        seen = jnp.int32(0)
        found = [jnp.int32(blocks)] * CAP
        for k in range(blocks):
            match = plan[behind, k] == target
            for c in range(CAP):
                found[c] = jnp.where(match & (seen == c), (k + stops - 1) % blocks, found[c])
            seen = seen + match.astype(jnp.int32)
        for c in range(CAP):
            picks[step, c] = found[c]
        return carry

    lax.fori_loop(0, lanes, find, 0)

    own = []
    for chunk in range(chunks):
        for k in range(blocks):
            pltpu.make_async_remote_copy(
                src_ref=gathered[chunk].at[k],
                dst_ref=gathered[chunk].at[k],
                send_sem=part_send.at[chunk, k],
                recv_sem=part_recv.at[chunk, k],
                device_id=(k, behind),
                device_id_type=MESH,
            ).wait_recv()
        for step in list(range(1, lanes)) + [0]:
            for c in range(CAP):
                staged[chunk, step, c] = gathered[chunk][picks[step, c]]
            if step > 0:
                slot_copy(chunk, step).start()
        own.append(
            pltpu.make_async_copy(
                staged.at[chunk, 0], received.at[:, slot_rows(chunk, lane)], own_sem.at[chunk]
            )
        )
        own[-1].start()
    for chunk in range(chunks):
        for step in range(1, lanes):
            sender = lax.rem(lane + step, lanes)
            pltpu.make_async_remote_copy(
                src_ref=staged.at[chunk, step],
                dst_ref=received.at[:, slot_rows(chunk, sender)],
                send_sem=slot_send.at[chunk, step],
                recv_sem=slot_recv.at[chunk, sender],
                device_id=(part_first + sender, group),
                device_id_type=MESH,
            ).wait_recv()
    for chunk in range(chunks):
        own[chunk].wait()
        for step in range(1, lanes):
            slot_copy(chunk, step).wait_send()
        for step in range(blocks):
            part_copy(chunk, step).wait_send()
        for stop in range(stops - 1):
            for half in range(2):
                ring_copy(stop, chunk, half).wait_send()
    save.wait()


def deliver(users, received, users_out, received_out, sem):
    tiles, slots = users.shape[0], received.shape[0]
    copies = [
        pltpu.make_async_copy(users.at[t], users_out.at[t], sem.at[t]) for t in range(tiles)
    ]
    for c in range(slots):
        copies.append(
            pltpu.make_async_copy(received.at[c], received_out.at[c], sem.at[tiles + c])
        )
    for copy in copies:
        copy.start()
    for copy in copies:
        copy.wait()


def shards(user_factors, item_factors, ratings, tile_rows, counts, plan):
    blocks, groups = lax.axis_size("blk"), lax.axis_size("group")
    _, _, stops, capt, tile, _ = ratings.shape
    _, rows, rank = user_factors.shape
    item_rows = item_factors.shape[1]
    parts = max(PARTS, blocks * 16 // item_rows)
    lanes = blocks // parts
    chunks = max(1, min(CHUNKS, item_rows // (lanes * 16)))
    width = item_rows // chunks
    depth = width // lanes
    tiled = (rows // tile, tile, rank)
    hbm = pl.BlockSpec(memory_space=pltpu.HBM)
    smem = pl.BlockSpec(memory_space=pltpu.SMEM)
    place = pl.BlockSpec(memory_space=pl.ANY)
    hops = max(stops - 1, 1)
    users, received = pl.pallas_call(
        functools.partial(kernel, blocks, groups, parts, chunks),
        out_shape=(
            jax.ShapeDtypeStruct(tiled, F32),
            jax.ShapeDtypeStruct((CAP, item_rows, rank), LOW),
        ),
        in_specs=[hbm, hbm, hbm, smem, smem, smem],
        out_specs=(place, place),
        scratch_shapes=[
            pltpu.VMEM(tiled, F32),
            pltpu.VMEM((item_rows, rank), F32),
            pltpu.VMEM(ratings.shape[2:], LOW),
            pltpu.VMEM((hops, chunks, 2, width, rank), LOW),
            pltpu.VMEM((hops, chunks, 2, width, rank), LOW),
            pltpu.VMEM((chunks, width, rank), LOW),
            pltpu.VMEM((chunks, lanes, CAP, depth, rank), LOW),
            pltpu.VMEM((capt + 1, tile, rank), F32),
            pltpu.SMEM((lanes, CAP), jnp.int32),
            pltpu.SemaphoreType.DMA((2 + stops,)),
            pltpu.SemaphoreType.DMA((hops, chunks, 2)),
            pltpu.SemaphoreType.DMA((hops, chunks, 2)),
            pltpu.SemaphoreType.DMA((chunks, blocks)),
            pltpu.SemaphoreType.DMA((chunks, blocks)),
            pltpu.SemaphoreType.DMA((chunks, lanes)),
            pltpu.SemaphoreType.DMA((chunks, lanes)),
            pltpu.SemaphoreType.DMA((chunks,)),
            pltpu.SemaphoreType.DMA,
        ]
        + [pltpu.VMEM((blocks + 1, depth, rank), LOW)] * chunks,
        compiler_params=pltpu.CompilerParams(
            collective_id=0, has_side_effects=True, vmem_limit_bytes=VMEM_GRANT
        ),
        cost_estimate=pl.CostEstimate(
            flops=6 * stops * capt * tile * item_rows * rank,
            bytes_accessed=2 * rows * rank * 4,
            transcendentals=0,
        ),
    )(
        user_factors.reshape(tiled),
        item_factors[0],
        ratings[0, 0],
        tile_rows[0, 0],
        counts[0, 0],
        plan,
    )
    users, received = pl.pallas_call(
        deliver,
        out_shape=(
            jax.ShapeDtypeStruct(tiled, F32),
            jax.ShapeDtypeStruct((CAP, item_rows, rank), LOW),
        ),
        in_specs=[place, place],
        out_specs=(hbm, hbm),
        scratch_shapes=[pltpu.SemaphoreType.DMA((tiled[0] + CAP,))],
        compiler_params=pltpu.CompilerParams(has_side_effects=True),
    )(users, received)
    return users.reshape(1, rows, rank), received[None, None]


def solution(mesh):
    in_specs = (
        P("group", "blk", None),
        P("group", "blk", None),
        P("group", "blk", None, None, None, None),
        P("group", "blk", None, None),
        P("group", "blk", None),
        P(),
    )
    out_specs = (P("group", "blk", None), P("group", "blk", None, None, None))
    return jax.shard_map(shards, mesh=mesh, in_specs=in_specs, out_specs=out_specs, check_vma=False)
```

```python
import functools

import jax
import jax.numpy as jnp
from jax import lax
from jax.experimental import pallas as pl
from jax.experimental.pallas import tpu as pltpu
from jax.sharding import PartitionSpec as P

CAP = 4
PARTS = 2
CHUNKS = 2
VMEM_GRANT = 63 * 1024 * 1024

learn_rate = 0.01
shrinkage = 0.05

MESH = pl.DeviceIdType.MESH
F32 = jnp.float32
LOW = jnp.bfloat16


def kernel(
    blocks, groups, parts, chunks,
    users_hbm, items_hbm, ratings_hbm, row_table, count_table, plan,
    users_out, received,
    users, items, ratings, ring_out, ring_in, handed, staged, change, picks,
    load_sem, ring_send, ring_recv, part_send, part_recv, slot_send, slot_recv, own_sem, out_sem,
    *gathered,
):
    stops, capt = ratings.shape[0], ratings.shape[1]
    tiles = users.shape[0]
    lanes = blocks // parts
    depth = gathered[0].shape[1]
    width = depth * lanes
    me = lax.axis_index("blk")
    group = lax.axis_index("group")
    ahead, behind = lax.rem(group + 1, groups), lax.rem(group + groups - 1, groups)
    right, left = lax.rem(me + 1, blocks), lax.rem(me + blocks - 1, blocks)
    part_first = (me // lanes) * lanes
    lane = me - part_first

    loads = [pltpu.make_async_copy(items_hbm, items, load_sem.at[0])]
    loads.append(pltpu.make_async_copy(users_hbm, users, load_sem.at[1]))
    for stop in range(stops):
        loads.append(
            pltpu.make_async_copy(ratings_hbm.at[stop], ratings.at[stop], load_sem.at[2 + stop])
        )
    for load in loads:
        load.start()

    barrier = pltpu.get_barrier_semaphore()
    pl.semaphore_signal(barrier, inc=1, device_id=(left, group), device_id_type=MESH)
    for step in range(blocks):
        pl.semaphore_signal(
            barrier, inc=1, device_id=(lax.rem(me + step, blocks), behind), device_id_type=MESH
        )
    for step in range(1, lanes):
        other = part_first + lax.rem(lane + step, lanes)
        pl.semaphore_signal(barrier, inc=1, device_id=(other, group), device_id_type=MESH)

    change[capt] = jnp.zeros(change.shape[1:], F32)
    for chunk in range(chunks):
        gathered[chunk][blocks] = jnp.zeros(gathered[chunk].shape[1:], LOW)

    def ring_copy(stop, chunk, half):
        return pltpu.make_async_remote_copy(
            src_ref=ring_out.at[stop, chunk, half],
            dst_ref=ring_in.at[stop, chunk, half],
            send_sem=ring_send.at[stop, chunk, half],
            recv_sem=ring_recv.at[stop, chunk, half],
            device_id=(right, group),
            device_id_type=MESH,
        )

    def part_copy(chunk, step):
        target = lax.rem(me + step, blocks)
        first = pl.multiple_of(lax.rem(target, lanes) * depth, depth)
        return pltpu.make_async_remote_copy(
            src_ref=handed.at[chunk, pl.ds(first, depth)],
            dst_ref=gathered[chunk].at[me],
            send_sem=part_send.at[chunk, step],
            recv_sem=part_recv.at[chunk, me],
            device_id=(target, ahead),
            device_id_type=MESH,
        )

    def slot_rows(chunk, holder):
        return pl.ds(pl.multiple_of(chunk * width + holder * depth, depth), depth)

    def slot_copy(chunk, step):
        return pltpu.make_async_remote_copy(
            src_ref=staged.at[chunk, step],
            dst_ref=received.at[:, slot_rows(chunk, lane)],
            send_sem=slot_send.at[chunk, step],
            recv_sem=slot_recv.at[chunk, lane],
            device_id=(part_first + lax.rem(lane + step, lanes), group),
            device_id_type=MESH,
        )

    loads[0].wait()
    loads[1].wait()
    for stop in range(stops):
        loads[2 + stop].wait()
        count = count_table[stop]
        active = [(c < count).astype(F32) for c in range(capt)]
        user_low = [users[row_table[stop, c]].astype(LOW) for c in range(capt)]
        kept = []
        for chunk in range(chunks):
            rows = slice(chunk * width, (chunk + 1) * width)
            if stop == 0:
                item_low = items[rows].astype(LOW)
            else:
                ring_copy(stop - 1, chunk, 0).wait_recv()
                item_low = ring_in[stop - 1, chunk, 0]
            grad = jnp.zeros((width, items.shape[1]), F32)
            residuals = []
            for c in range(capt):
                predicted = lax.dot_general(
                    user_low[c], item_low, (((1,), (1,)), ((), ())), preferred_element_type=F32
                )
                residual = (
                    active[c] * (ratings[stop, c, :, rows].astype(F32) - predicted)
                ).astype(LOW)
                grad = grad + lax.dot_general(
                    residual, user_low[c], (((0,), (0,)), ((), ())), preferred_element_type=F32
                )
                residuals.append(residual)
            kept.append((item_low, residuals))
            if stop == 0:
                block = items[rows]
            else:
                ring_copy(stop - 1, chunk, 1).wait_recv()
                block = item_low.astype(F32) + ring_in[stop - 1, chunk, 1].astype(F32)
            block = block + learn_rate * (grad - shrinkage * count.astype(F32) * block)
            if stop == 0 and chunk == 0:
                pl.semaphore_wait(barrier, blocks + lanes)
            if stop < stops - 1:
                high = block.astype(LOW)
                ring_out[stop, chunk, 0] = high
                ring_copy(stop, chunk, 0).start()
                ring_out[stop, chunk, 1] = (block - high.astype(F32)).astype(LOW)
                ring_copy(stop, chunk, 1).start()
            else:
                handed[chunk] = block.astype(LOW)
                for step in range(blocks):
                    part_copy(chunk, step).start()
        for c in range(capt):
            before = users[row_table[stop, c]]
            user_step = jnp.zeros(before.shape, F32)
            for item_low, residuals in kept:
                user_step = user_step + jnp.dot(
                    residuals[c], item_low, preferred_element_type=F32
                )
            change[c] = learn_rate * active[c] * (user_step - shrinkage * before)
        for tile in range(tiles):
            which = jnp.int32(capt)
            for c in range(capt):
                which = jnp.where(row_table[stop, c] == tile, c, which)
            users[tile] = users[tile] + change[which]
    save = pltpu.make_async_copy(users, users_out, out_sem)
    save.start()

    def find(step, carry):
        target = part_first + lax.rem(lane + step, lanes)
        seen = jnp.int32(0)
        found = [jnp.int32(blocks)] * CAP
        for k in range(blocks):
            match = plan[behind, k] == target
            for c in range(CAP):
                found[c] = jnp.where(match & (seen == c), (k + stops - 1) % blocks, found[c])
            seen = seen + match.astype(jnp.int32)
        for c in range(CAP):
            picks[step, c] = found[c]
        return carry

    lax.fori_loop(0, lanes, find, 0)

    own = []
    for chunk in range(chunks):
        for k in range(blocks):
            pltpu.make_async_remote_copy(
                src_ref=gathered[chunk].at[k],
                dst_ref=gathered[chunk].at[k],
                send_sem=part_send.at[chunk, k],
                recv_sem=part_recv.at[chunk, k],
                device_id=(k, behind),
                device_id_type=MESH,
            ).wait_recv()
        for step in list(range(1, lanes)) + [0]:
            for c in range(CAP):
                staged[chunk, step, c] = gathered[chunk][picks[step, c]]
            if step > 0:
                slot_copy(chunk, step).start()
        own.append(
            pltpu.make_async_copy(
                staged.at[chunk, 0], received.at[:, slot_rows(chunk, lane)], own_sem.at[chunk]
            )
        )
        own[-1].start()
    for chunk in range(chunks):
        for step in range(1, lanes):
            sender = lax.rem(lane + step, lanes)
            pltpu.make_async_remote_copy(
                src_ref=staged.at[chunk, step],
                dst_ref=received.at[:, slot_rows(chunk, sender)],
                send_sem=slot_send.at[chunk, step],
                recv_sem=slot_recv.at[chunk, sender],
                device_id=(part_first + sender, group),
                device_id_type=MESH,
            ).wait_recv()
    for chunk in range(chunks):
        own[chunk].wait()
        for step in range(1, lanes):
            slot_copy(chunk, step).wait_send()
        for step in range(blocks):
            part_copy(chunk, step).wait_send()
        for stop in range(stops - 1):
            for half in range(2):
                ring_copy(stop, chunk, half).wait_send()
    save.wait()


def deliver(users, received, users_out, received_out, users_held, slots_held, in_sem, out_sem):
    tiles, slots = users.shape[0], received.shape[0]
    moves = [(users, users_held, users_out, t) for t in range(tiles)]
    moves += [(received, slots_held, received_out, c) for c in range(slots)]
    ins, outs = [], []
    for i, (source, held, target, at) in enumerate(moves):
        ins.append(pltpu.make_async_copy(source.at[at], held.at[at], in_sem.at[i]))
        outs.append(pltpu.make_async_copy(held.at[at], target.at[at], out_sem.at[i]))
    for copy in ins:
        copy.start()
    for copy_in, copy_out in zip(ins, outs):
        copy_in.wait()
        copy_out.start()
    for copy in outs:
        copy.wait()


def shards(user_factors, item_factors, ratings, tile_rows, counts, plan):
    blocks, groups = lax.axis_size("blk"), lax.axis_size("group")
    _, _, stops, capt, tile, _ = ratings.shape
    _, rows, rank = user_factors.shape
    item_rows = item_factors.shape[1]
    parts = max(PARTS, blocks * 16 // item_rows)
    lanes = blocks // parts
    chunks = max(1, min(CHUNKS, item_rows // (lanes * 16)))
    width = item_rows // chunks
    depth = width // lanes
    tiled = (rows // tile, tile, rank)
    hbm = pl.BlockSpec(memory_space=pltpu.HBM)
    smem = pl.BlockSpec(memory_space=pltpu.SMEM)
    place = pl.BlockSpec(memory_space=pl.ANY)
    hops = max(stops - 1, 1)
    users, received = pl.pallas_call(
        functools.partial(kernel, blocks, groups, parts, chunks),
        out_shape=(
            jax.ShapeDtypeStruct(tiled, F32),
            jax.ShapeDtypeStruct((CAP, item_rows, rank), LOW),
        ),
        in_specs=[hbm, hbm, hbm, smem, smem, smem],
        out_specs=(place, place),
        scratch_shapes=[
            pltpu.VMEM(tiled, F32),
            pltpu.VMEM((item_rows, rank), F32),
            pltpu.VMEM(ratings.shape[2:], LOW),
            pltpu.VMEM((hops, chunks, 2, width, rank), LOW),
            pltpu.VMEM((hops, chunks, 2, width, rank), LOW),
            pltpu.VMEM((chunks, width, rank), LOW),
            pltpu.VMEM((chunks, lanes, CAP, depth, rank), LOW),
            pltpu.VMEM((capt + 1, tile, rank), F32),
            pltpu.SMEM((lanes, CAP), jnp.int32),
            pltpu.SemaphoreType.DMA((2 + stops,)),
            pltpu.SemaphoreType.DMA((hops, chunks, 2)),
            pltpu.SemaphoreType.DMA((hops, chunks, 2)),
            pltpu.SemaphoreType.DMA((chunks, blocks)),
            pltpu.SemaphoreType.DMA((chunks, blocks)),
            pltpu.SemaphoreType.DMA((chunks, lanes)),
            pltpu.SemaphoreType.DMA((chunks, lanes)),
            pltpu.SemaphoreType.DMA((chunks,)),
            pltpu.SemaphoreType.DMA,
        ]
        + [pltpu.VMEM((blocks + 1, depth, rank), LOW)] * chunks,
        compiler_params=pltpu.CompilerParams(
            collective_id=0, has_side_effects=True, vmem_limit_bytes=VMEM_GRANT
        ),
        cost_estimate=pl.CostEstimate(
            flops=6 * stops * capt * tile * item_rows * rank,
            bytes_accessed=2 * rows * rank * 4,
            transcendentals=0,
        ),
    )(
        user_factors.reshape(tiled),
        item_factors[0],
        ratings[0, 0],
        tile_rows[0, 0],
        counts[0, 0],
        plan,
    )
    users, received = pl.pallas_call(
        deliver,
        out_shape=(
            jax.ShapeDtypeStruct(tiled, F32),
            jax.ShapeDtypeStruct((CAP, item_rows, rank), LOW),
        ),
        in_specs=[place, place],
        out_specs=(hbm, hbm),
        scratch_shapes=[
            pltpu.VMEM(tiled, F32),
            pltpu.VMEM((CAP, item_rows, rank), LOW),
            pltpu.SemaphoreType.DMA((tiled[0] + CAP,)),
            pltpu.SemaphoreType.DMA((tiled[0] + CAP,)),
        ],
        compiler_params=pltpu.CompilerParams(vmem_limit_bytes=VMEM_GRANT),
    )(users, received)
    return users.reshape(1, rows, rank), received[None, None]


def solution(mesh):
    in_specs = (
        P("group", "blk", None),
        P("group", "blk", None),
        P("group", "blk", None, None, None, None),
        P("group", "blk", None, None),
        P("group", "blk", None),
        P(),
    )
    out_specs = (P("group", "blk", None), P("group", "blk", None, None, None))
    return jax.shard_map(shards, mesh=mesh, in_specs=in_specs, out_specs=out_specs, check_vma=False)
```
